512 devices in a mesh: dp: 32 (over z_lo, x), fsdp: 16 (over z_hi, y, core).
Axes of the slice: x: 4, y: 4, z: 16 (z_hi: 2, z_lo: 8; z = z_hi * 8 + z_lo), core: 2. Of those that a mesh axis runs over, the one named last changes fastest.
Arguments:
- hidden_in: bfloat16 [65536, 8192], P(('dp', 'fsdp')), may hold values from -6 to 6
- norm_gain: bfloat16 [8192], P('fsdp'), may hold values from 0.099609375 to 1.8984375
- value_grad: bfloat16 [65536, 512], P(('dp', 'fsdp')), may hold values from -6 to 6
- value_weight: bfloat16 [8192, 512], P('fsdp'), may hold values from -0.25 to 0.25
- proj_input: bfloat16 [8192, 64], P('fsdp'), may hold values from -0.0014648438 to 0.0014648438
- proj_output: bfloat16 [512, 64], replicated, may hold values from -0.25 to 0.25
- query_feats: float32 [1024, 4096], P(('dp', 'fsdp')), may hold values from -0.09375 to 0.09375
- example_slot: int32 [32], replicated, may hold values from 0 to 31, each once
Outputs:
- input_grad: bfloat16 [65536, 8192], P(('dp', 'fsdp'))
- gram_matrix: float32 [4096, 4096], P('dp', 'fsdp')
- scores: float32 [32, 1024], P(None, ('dp', 'fsdp'))
The draws below stay inside these ranges and needn't reach their ends.
Inputs may be any that keep to these rules, and one draw needn't show every extreme that they name: `example_slot`: each example number appears once.
All inputs are finite; a program needn't handle non-finite values.
Results may differ from the reference program's by a relative error of at most 0.012.
Values may be sent and summed in bfloat16 or wider, within the bound.
No kernel may reach another device: no remote copies, remote signals or barrier semaphores. Data moves between devices by JAX's collectives and lax.ppermute only.
A program may use at most 64 MiB of HBM per device.

```python
import jax
import jax.numpy as jnp
from jax import lax

D = 8192
KV = 512
PROJ = 64
QUERIES = 1024
TOK_DEV = 128
EXAMPLES = 32
TOKENS = 65536
FEAT = 4096
N_FSDP = 16


def block_scale(key, dims, cuts, least, top_value):
    gain = 1.0
    for axis_at, shards_of in cuts:
        draws = jax.random.uniform(jax.random.fold_in(jax.random.fold_in(key, 6), axis_at), (shards_of,), jnp.float32, least / len(cuts), top_value / len(cuts))
        gain = gain * jnp.repeat(jnp.exp(draws), dims[axis_at] // shards_of).reshape((-1,) + (1,) * (len(dims) - 1 - axis_at))
    return gain


def scatter_about(own_key, extent, width, limit, pieces=(), dtype=jnp.bfloat16):
    result = width * jax.random.normal(own_key, extent, jnp.float32)
    if pieces:
        result = result * block_scale(own_key, extent, pieces, -0.22, 0.18)
    return jnp.clip(result, -limit, limit).astype(dtype)


def setup_inputs(seed: int = 0) -> dict:
    splits = jax.random.split(jax.random.key(seed), 9)
    hidden_in = scatter_about(splits[0], (TOKENS, D), 1.0, 6.0, ((0, 512),))
    norm_gain = jnp.clip(1.0 + 0.18 * jax.random.normal(splits[1], (D,), jnp.float32), 0.099609375, 1.8984375).astype(jnp.bfloat16)
    value_grad = scatter_about(splits[2], (TOKENS, KV), 1.0, 6.0, ((0, 512),))
    value_weight = scatter_about(splits[3], (D, KV), KV ** -0.5, 0.25, ((0, 16),))
    proj_input = scatter_about(splits[4], (D, PROJ), (D * TOK_DEV * N_FSDP) ** -0.5, 0.0014648438, ((0, 16),))
    proj_output = scatter_about(splits[5], (KV, PROJ), KV ** -0.5, 0.25)
    query_feats = scatter_about(splits[6], (QUERIES, FEAT), FEAT ** -0.5, 0.09375, ((0, 512),), jnp.float32)
    example_slot = jax.random.permutation(splits[7], EXAMPLES).astype(jnp.int32)
    return dict(hidden_in=hidden_in, norm_gain=norm_gain, value_grad=value_grad, value_weight=value_weight, proj_input=proj_input, proj_output=proj_output, query_feats=query_feats, example_slot=example_slot)


def one_example(packed, gain_wide, value_weight, proj_input, proj_output):
    hidden_in, value_grad = packed
    wide_x = hidden_in.astype(jnp.float32)
    inverse_rms = lax.rsqrt(lax.optimization_barrier(jnp.mean(wide_x * wide_x, axis=-1, keepdims=True)) + 1e-05)
    normed = (wide_x * inverse_rms * gain_wide).astype(jnp.bfloat16)
    dnormed = jnp.dot(value_grad, value_weight.T, preferred_element_type=jnp.float32).astype(jnp.bfloat16)
    scaled = dnormed.astype(jnp.float32) * gain_wide
    inner_sum = lax.optimization_barrier(jnp.sum(scaled * wide_x, axis=-1, keepdims=True))
    input_grad = (scaled * inverse_rms - wide_x * inner_sum * inverse_rms ** 3 / D).astype(jnp.bfloat16)
    left_proj = jnp.dot(normed, proj_input, preferred_element_type=jnp.float32).astype(jnp.bfloat16)
    right_proj = jnp.dot(value_grad, proj_output, preferred_element_type=jnp.float32).astype(jnp.bfloat16)
    feats = jnp.dot(left_proj.T, right_proj, preferred_element_type=jnp.float32).reshape(FEAT)
    return (input_grad, feats)

def reference(hidden_in, norm_gain, value_grad, value_weight, proj_input, proj_output, query_feats, example_slot):
    length = TOK_DEV * N_FSDP
    gain_wide = norm_gain.astype(jnp.float32)
    blocks = (hidden_in.reshape(EXAMPLES, length, D), value_grad.reshape(EXAMPLES, length, KV))
    input_grad, feats = lax.map(lambda packed: one_example(packed, gain_wide, value_weight, proj_input, proj_output), blocks)
    input_grad = input_grad.reshape(TOKENS, D)

    def add_term(total, vector):
        outer_terms = (vector[:, None] * vector[None, :]).astype(jnp.bfloat16)
        outer_terms = lax.optimization_barrier(outer_terms)
        return (total + outer_terms.astype(jnp.float32), None)
    gram_matrix, _ = lax.scan(add_term, jnp.zeros((FEAT, FEAT), jnp.float32), feats)
    raw_scores = jnp.dot(feats, query_feats.T, precision=lax.Precision.HIGHEST)
    scores = jnp.zeros((EXAMPLES, QUERIES), jnp.float32).at[example_slot.astype(jnp.int32)].set(raw_scores)
    return (input_grad, gram_matrix, scores)
```

```python
import jax
import jax.numpy as jnp
from jax import lax
from jax.experimental import pallas as pl
from jax.experimental.pallas import tpu as pltpu
from jax.sharding import Mesh, PartitionSpec as P

F32 = jnp.float32
BF16 = jnp.bfloat16

NAMES = ("zlo", "x", "zhi", "y", "core")
DP = ("zlo", "x")
FSDP = ("zhi", "y", "core")
NEAR = ("y", "core")

NT = (((1,), (1,)), ((), ()))
TN = (((0,), (0,)), ((), ()))
VMEM = pl.BlockSpec(memory_space=pltpu.VMEM)
SMEM = pl.BlockSpec(memory_space=pltpu.SMEM)
HBM = pl.BlockSpec(memory_space=pltpu.HBM)
PARAMS = pltpu.CompilerParams(vmem_limit_bytes=24 * 1024 * 1024)


def shape(dims, dtype):
    return jax.ShapeDtypeStruct(dims, dtype)


def cost(flops, traffic):
    return pl.CostEstimate(flops=flops, bytes_accessed=traffic, transcendentals=0)


def lane_sum(value):
    total = value[:, :128]
    for at in range(128, value.shape[1], 128):
        total = total + value[:, at : at + 128]
    return total


def fold_gain(x_ref, gain_ref, p_ref, w_ref, send_ref, weight_ref):
    proj = p_ref.shape[0]
    piece = send_ref.shape[0] - proj
    gain = gain_ref[...].astype(F32)
    send_ref[:proj] = (p_ref[...].astype(F32) * gain).astype(BF16)
    for at in range(0, w_ref.shape[0], piece):
        wide = jnp.broadcast_to(gain[:, at : at + piece], (8, piece))
        column = wide.T[:, :1]
        rows = slice(at, at + piece)
        weight_ref[rows, :] = (w_ref[rows, :].astype(F32) * column).astype(BF16)
    send_ref[proj:] = weight_ref[pl.ds(pl.multiple_of(x_ref[0] * piece, piece), piece), :]


def pair_factors(send_ref, recv_ref, out_ref, rows_ref, pair_ref, sem):
    proj = pair_ref.shape[0] // 2
    pair_ref[:proj] = send_ref[:proj]
    pair_ref[proj:] = recv_ref[:proj]
    copies = [
        pltpu.make_async_copy(pair_ref, out_ref.at[at], sem.at[at])
        for at in range(out_ref.shape[0])
    ]
    for copy in copies:
        copy.start()
    rows_ref[...] = recv_ref[proj:]
    for copy in copies:
        copy.wait()


def token_stats(x_ref, v_ref, po_ref, inv_ref, right_ref):
    rows, width = x_ref.shape
    step = 512

    def body(at, acc):
        part = x_ref[:, pl.ds(pl.multiple_of(at * step, step), step)].astype(F32)
        return acc + lane_sum(part * part)

    acc = lax.fori_loop(0, width // step, body, jnp.zeros((rows, 128), F32))
    mean = jnp.sum(acc, axis=1, keepdims=True) / width
    inv_ref[...] = jnp.broadcast_to(lax.rsqrt(mean + 1e-05), inv_ref.shape)
    right_ref[...] = lax.dot_general(
        v_ref[...], po_ref[...], NT, preferred_element_type=F32
    ).astype(BF16)


def partial_feats(zhi_ref, x_ref, g_ref, inv_ref, right_ref, out_ref, rows_ref):
    near, both, depth = g_ref.shape
    proj = both // 2
    zhi = zhi_ref[0]
    acc = jnp.zeros((x_ref.shape[0], proj), F32)
    for half in range(2):
        first = (zhi if half == 0 else 1 - zhi) * near
        for at in range(near):
            cols = pl.ds(pl.multiple_of((first + at) * depth, depth), depth)
            acc = acc + lax.dot_general(
                x_ref[:, cols], g_ref[at, half * proj : (half + 1) * proj, :], NT,
                preferred_element_type=F32,
            )
    left = (acc * inv_ref[:, :1]).astype(BF16)
    rows_ref[...] = lax.dot_general(left, right_ref[...], TN, preferred_element_type=F32)
    even = rows_ref[pl.ds(0, proj // 2, stride=2), :]
    odd = rows_ref[pl.ds(1, proj // 2, stride=2), :]
    both = jnp.concatenate([even, odd], axis=1)
    for at in range(out_ref.shape[0]):
        out_ref[at] = both


def add_partials(parts_ref, out_ref):
    own = jnp.sum(parts_ref[...], axis=0).astype(BF16)
    for at in range(out_ref.shape[0]):
        out_ref[at] = own


def finish(place_ref, tab_ref, q_ref, slot_ref, gram_ref, score_ref, wide_ref):
    count = tab_ref.shape[0]
    wide_ref[...] = tab_ref[...].astype(F32)
    row, col = place_ref[0], place_ref[1]
    rows = wide_ref[:, row, :].astype(BF16)
    for k in range(2):
        cols = wide_ref[:, 2 * col + k, :].astype(BF16)
        gram_ref[:, k * 128 : (k + 1) * 128] = lax.dot_general(
            rows, cols, TN, preferred_element_type=F32
        )
    hit = slot_ref[...] == lax.broadcasted_iota(jnp.int32, (count, count), 1)
    for k in range(q_ref.shape[0]):
        terms = jnp.sum(wide_ref[...] * q_ref[k][None], axis=1)
        raw = jnp.sum(terms, axis=1, keepdims=True)
        score_ref[k : k + 1, :] = jnp.sum(jnp.where(hit, raw, 0.0), axis=0, keepdims=True)


def half_product(first, turn, x_ref, v_ref, w_ref, s_ref, held_ref, sem, acc):
    near, depth, _ = w_ref.shape
    copies = [
        pltpu.make_async_copy(w_ref.at[at], held_ref.at[at], sem.at[at]) for at in range(near)
    ]
    for copy in copies:
        copy.start()
    for at in range(near):
        copies[at].wait()
        scaled = lax.dot_general(v_ref[...], held_ref[at], NT, preferred_element_type=F32)
        s_ref[:, at * depth : (at + 1) * depth] = scaled
        for k in range(depth // 128):
            source = k if turn is None else turn[k]
            cols = pl.ds(pl.multiple_of((first + at) * depth + source * 128, 128), 128)
            acc = acc + scaled[:, k * 128 : (k + 1) * 128] * x_ref[:, cols].astype(F32)
    return acc


def near_half(spot_ref, x_ref, v_ref, w_ref, s_ref, inner_ref, held_ref, sem):
    first = spot_ref[1] * w_ref.shape[0]
    inner_ref[...] = half_product(
        first, None, x_ref, v_ref, w_ref, s_ref, held_ref, sem, jnp.zeros(inner_ref.shape, F32)
    )


def far_half(
    spot_ref, x_ref, v_ref, w_ref, s_ref, inner_ref, inv_ref, o_ref,
    held_ref, sem, far_ref, out_ref, out_sem,
):
    near, depth, _ = w_ref.shape
    width = x_ref.shape[1]
    x_at, zhi = spot_ref[0], spot_ref[1]
    across = depth // 128
    turn = [lax.rem(x_at - hop + across, across) for hop in range(across)]
    acc = half_product(
        (1 - zhi) * near, turn, x_ref, v_ref, w_ref, far_ref, held_ref, sem, inner_ref[...]
    )
    inv = inv_ref[:, :1]
    factor = jnp.sum(acc, axis=1, keepdims=True) * inv * inv * inv / width
    copies = []
    for half, source, order in ((zhi, s_ref, range(across)), (1 - zhi, far_ref, turn)):
        for at in range(near):
            start = (half * near + at) * depth
            slot = len(copies)
            for k in range(across):
                here = slice(at * depth + k * 128, at * depth + (k + 1) * 128)
                cols = pl.ds(pl.multiple_of(start + order[k] * 128, 128), 128)
                value = source[:, here] * inv - x_ref[:, cols].astype(F32) * factor
                out_ref[slot, :, pl.ds(pl.multiple_of(order[k] * 128, 128), 128)] = value.astype(
                    BF16
                )
            cols = pl.ds(pl.multiple_of(start, depth), depth)
            copy = pltpu.make_async_copy(out_ref.at[slot], o_ref.at[:, cols], out_sem.at[slot])
            copy.start()
            copies.append(copy)
    for copy in copies:
        copy.wait()


def local(
    hidden_in,
    norm_gain,
    value_grad,
    value_weight,
    proj_input,
    proj_output,
    query_feats,
    example_slot,
):
    tokens, width = hidden_in.shape
    depth, feats = value_weight.shape
    proj = proj_input.shape[1]
    lines = proj * proj // 128
    examples = lax.axis_size(DP)
    group = lax.axis_size(FSDP)
    near = group // 2
    across = lax.axis_size("x")
    piece = depth // across
    zhi = lax.axis_index("zhi").astype(jnp.int32).reshape(1)
    x_at = lax.axis_index("x").astype(jnp.int32).reshape(1)
    spot = jnp.concatenate([x_at, zhi])

    send, weight = pl.pallas_call(
        fold_gain,
        out_shape=(shape((proj + piece, depth), BF16), shape((depth, feats), BF16)),
        in_specs=[SMEM] + [VMEM] * 3,
        out_specs=(VMEM, VMEM),
        compiler_params=PARAMS,
    )(x_at, norm_gain.reshape(1, depth), proj_input.T, value_weight)
    weight_near = lax.all_gather(weight, NEAR, axis=0)
    recv = lax.ppermute(send, "zhi", [(0, 1), (1, 0)])
    pairs, rows_far = pl.pallas_call(
        pair_factors,
        out_shape=(shape((near, 2 * proj, depth), BF16), shape((piece, feats), BF16)),
        in_specs=[VMEM] * 2,
        out_specs=(HBM, VMEM),
        scratch_shapes=[
            pltpu.VMEM((2 * proj, depth), BF16),
            pltpu.SemaphoreType.DMA((near,)),
        ],
        compiler_params=PARAMS,
    )(send, recv)
    pairs = lax.all_to_all(pairs, NEAR, 0, 0, tiled=True)

    inv, right = pl.pallas_call(
        token_stats,
        out_shape=(shape((tokens, 128), F32), shape((tokens, proj), BF16)),
        in_specs=[VMEM] * 3,
        out_specs=(VMEM, VMEM),
        compiler_params=PARAMS,
        cost_estimate=cost(2 * tokens * width, 2 * tokens * width),
    )(hidden_in, value_grad, proj_output.T)

    rows_far, inv = lax.optimization_barrier((rows_far, inv))
    moved = [rows_far] + [
        lax.ppermute(rows_far, "x", [(i, (i + hop) % across) for i in range(across)])
        for hop in range(1, across)
    ]
    weight_far = lax.all_gather(jnp.concatenate(moved, axis=0), NEAR, axis=0)

    partial = pl.pallas_call(
        partial_feats,
        out_shape=shape((group, lines, 128), F32),
        in_specs=[SMEM] + [VMEM] * 4,
        out_specs=VMEM,
        scratch_shapes=[pltpu.VMEM((proj, proj), F32)],
        compiler_params=PARAMS,
    )(zhi, hidden_in, pairs, inv, right)
    partial, weight_near = lax.optimization_barrier((partial, weight_near))
    partials = lax.all_to_all(partial, FSDP, 0, 0, tiled=True)
    near_scaled, near_inner = pl.pallas_call(
        near_half,
        out_shape=(shape((tokens, near * depth), F32), shape((tokens, 128), F32)),
        in_specs=[SMEM, VMEM, VMEM, HBM],
        out_specs=(VMEM, VMEM),
        scratch_shapes=[
            pltpu.VMEM((near, depth, feats), BF16),
            pltpu.SemaphoreType.DMA((near,)),
        ],
        compiler_params=PARAMS,
        cost_estimate=cost(tokens * feats * width, feats * width),
    )(spot, hidden_in, value_grad, weight_near)
    partials, near_inner = lax.optimization_barrier((partials, near_inner))

    own = pl.pallas_call(
        add_partials,
        out_shape=shape((examples, lines, 128), BF16),
        in_specs=[VMEM],
        out_specs=VMEM,
        compiler_params=PARAMS,
    )(partials)
    table = lax.all_to_all(own, DP, 0, 0, tiled=True)
    input_grad = pl.pallas_call(
        far_half,
        out_shape=shape((tokens, width), BF16),
        in_specs=[SMEM, VMEM, VMEM, HBM, VMEM, VMEM, VMEM],
        out_specs=HBM,
        scratch_shapes=[
            pltpu.VMEM((near, depth, feats), BF16),
            pltpu.SemaphoreType.DMA((near,)),
            pltpu.VMEM((tokens, near * depth), F32),
            pltpu.VMEM((group, tokens, depth), BF16),
            pltpu.SemaphoreType.DMA((group,)),
        ],
        compiler_params=PARAMS,
        cost_estimate=cost(tokens * feats * width, 2 * feats * width),
    )(spot, hidden_in, value_grad, weight_far, near_scaled, near_inner, inv)

    place = jnp.stack([lax.axis_index(DP), lax.axis_index(FSDP)]).astype(jnp.int32)
    gram, score = pl.pallas_call(
        finish,
        out_shape=(
            shape((proj * proj // examples, proj * proj // group), F32),
            shape((query_feats.shape[0], examples), F32),
        ),
        in_specs=[SMEM] + [VMEM] * 3,
        out_specs=(VMEM, VMEM),
        scratch_shapes=[pltpu.VMEM((examples, lines, 128), F32)],
        compiler_params=PARAMS,
    )(place, table, query_feats.reshape(-1, lines, 128), example_slot.reshape(examples, 1))

    return (input_grad, gram, score.T)


def solution(mesh):
    fine = Mesh(mesh.devices.reshape(8, 4, 2, 4, 2), NAMES)
    return jax.shard_map(
        local,
        mesh=fine,
        in_specs=(
            P(NAMES, None),
            P(FSDP),
            P(NAMES, None),
            P(FSDP, None),
            P(FSDP, None),
            P(),
            P(NAMES, None),
            P(),
        ),
        out_specs=(P(NAMES, None), P(DP, FSDP), P(None, NAMES)),
        check_vma=False,
    )
```

```python
import jax
import jax.numpy as jnp
from jax import lax
from jax.experimental import pallas as pl
from jax.experimental.pallas import tpu as pltpu
from jax.sharding import Mesh, PartitionSpec as P

F32 = jnp.float32
BF16 = jnp.bfloat16

NAMES = ("zlo", "x", "zhi", "y", "core")
DP = ("zlo", "x")
FSDP = ("zhi", "y", "core")
NEAR = ("y", "core")

NT = (((1,), (1,)), ((), ()))
TN = (((0,), (0,)), ((), ()))
VMEM = pl.BlockSpec(memory_space=pltpu.VMEM)
SMEM = pl.BlockSpec(memory_space=pltpu.SMEM)
HBM = pl.BlockSpec(memory_space=pltpu.HBM)
LARGE = pltpu.CompilerParams(vmem_limit_bytes=56 * 1024 * 1024)
PARAMS = pltpu.CompilerParams(vmem_limit_bytes=24 * 1024 * 1024)


def shape(dims, dtype):
    return jax.ShapeDtypeStruct(dims, dtype)


def cost(flops, traffic):
    return pl.CostEstimate(flops=flops, bytes_accessed=traffic, transcendentals=0)


def lane_sum(value):
    total = value[:, :128]
    for at in range(128, value.shape[1], 128):
        total = total + value[:, at : at + 128]
    return total


def token_stats(x_ref, v_ref, po_ref, inv_ref, right_ref):
    rows, width = x_ref.shape
    step = 512

    def body(at, acc):
        part = x_ref[:, pl.ds(pl.multiple_of(at * step, step), step)].astype(F32)
        return acc + lane_sum(part * part)

    acc = lax.fori_loop(0, width // step, body, jnp.zeros((rows, 128), F32))
    mean = jnp.sum(acc, axis=1, keepdims=True) / width
    inv_ref[...] = jnp.broadcast_to(lax.rsqrt(mean + 1e-05), inv_ref.shape)
    right_ref[...] = lax.dot_general(
        v_ref[...], po_ref[...], NT, preferred_element_type=F32
    ).astype(BF16)


def partial_feats(zhi_ref, x_ref, g_ref, inv_ref, right_ref, out_ref, rows_ref):
    near, both, depth = g_ref.shape
    proj = (both - 16) // 2
    zhi = zhi_ref[0]
    acc = jnp.zeros((x_ref.shape[0], proj), F32)
    for half in range(2):
        first = (zhi if half == 0 else 1 - zhi) * near
        for at in range(near):
            cols = pl.ds(pl.multiple_of((first + at) * depth, depth), depth)
            acc = acc + lax.dot_general(
                x_ref[:, cols], g_ref[at, half * proj : (half + 1) * proj, :], NT,
                preferred_element_type=F32,
            )
    left = (acc * inv_ref[:, :1]).astype(BF16)
    rows_ref[...] = lax.dot_general(left, right_ref[...], TN, preferred_element_type=F32)
    even = rows_ref[pl.ds(0, proj // 2, stride=2), :]
    odd = rows_ref[pl.ds(1, proj // 2, stride=2), :]
    out_ref[...] = jnp.concatenate([even, odd], axis=1)


def finish(place_ref, tab_ref, q_ref, slot_ref, gram_ref, score_ref, wide_ref):
    count = tab_ref.shape[0]
    wide_ref[...] = tab_ref[...].astype(F32)
    row, col = place_ref[0], place_ref[1]
    rows = wide_ref[:, row, :].astype(BF16)
    for k in range(2):
        cols = wide_ref[:, 2 * col + k, :].astype(BF16)
        gram_ref[:, k * 128 : (k + 1) * 128] = lax.dot_general(
            rows, cols, TN, preferred_element_type=F32
        )
    hit = slot_ref[...] == lax.broadcasted_iota(jnp.int32, (count, count), 1)
    for k in range(q_ref.shape[0]):
        terms = jnp.sum(wide_ref[...] * q_ref[k][None], axis=1)
        raw = jnp.sum(terms, axis=1, keepdims=True)
        score_ref[k : k + 1, :] = jnp.sum(jnp.where(hit, raw, 0.0), axis=0, keepdims=True)


def half_product(first, order, x_ref, v_ref, w_ref, g_ref, row, s_ref, held_ref, sem, acc):
    near, depth, _ = w_ref.shape
    copies = [
        pltpu.make_async_copy(w_ref.at[at], held_ref.at[at], sem.at[at]) for at in range(near)
    ]
    for copy in copies:
        copy.start()
    for at in range(near):
        copies[at].wait()
        product = lax.dot_general(v_ref[...], held_ref[at], NT, preferred_element_type=F32)
        for k in range(depth // 128):
            part = order[k] * 128
            part = part if isinstance(part, int) else pl.multiple_of(part, 128)
            gain = g_ref[at, row : row + 8, pl.ds(part, 128)][:1].astype(F32)
            scaled = product[:, k * 128 : (k + 1) * 128] * gain
            s_ref[at, :, pl.ds(part, 128)] = scaled.astype(s_ref.dtype)
            cols = pl.ds(pl.multiple_of((first + at) * depth + part, 128), 128)
            acc = acc + scaled * x_ref[:, cols].astype(F32)
    return acc


def near_half(spot_ref, x_ref, v_ref, g_ref, w_ref, s_ref, inner_ref, held_ref, sem):
    near, depth, _ = w_ref.shape
    inner_ref[...] = half_product(
        spot_ref[1] * near, range(depth // 128), x_ref, v_ref, w_ref, g_ref, g_ref.shape[1] - 16,
        s_ref, held_ref, sem, jnp.zeros(inner_ref.shape, F32),
    )


def input_gradient(
    spot_ref, x_ref, v_ref, g_ref, w_ref, s_ref, inner_ref, inv_ref, o_ref,
    held_ref, sem, far_ref, out_ref, out_sem,
):
    near, depth, _ = w_ref.shape
    width = x_ref.shape[1]
    across = depth // 128
    zhi = spot_ref[1]
    turn = [lax.rem(spot_ref[0] - hop + across, across) for hop in range(across)]
    acc = half_product(
        (1 - zhi) * near, turn, x_ref, v_ref, w_ref, g_ref, g_ref.shape[1] - 8,
        far_ref, held_ref, sem, inner_ref[...],
    )
    inv = inv_ref[...]
    total = jnp.broadcast_to(jnp.sum(acc, axis=1, keepdims=True), inv.shape)
    factor = total * inv * inv * inv / width
    stores = []
    for slot in range(2 * near):
        half, at = divmod(slot, near)
        source = s_ref if half == 0 else far_ref
        first = ((zhi if half == 0 else 1 - zhi) * near + at) * depth
        cols = pl.ds(pl.multiple_of(first, depth), depth)
        for k in range(across):
            here = slice(k * 128, (k + 1) * 128)
            some = pl.ds(pl.multiple_of(first + k * 128, 128), 128)
            out_ref[slot, :, here] = (
                source[at, :, here].astype(F32) * inv - x_ref[:, some].astype(F32) * factor
            ).astype(BF16)
        copy = pltpu.make_async_copy(out_ref.at[slot], o_ref.at[:, cols], out_sem.at[slot])
        copy.start()
        stores.append(copy)
    for copy in stores:
        copy.wait()


def local(
    hidden_in,
    norm_gain,
    value_grad,
    value_weight,
    proj_input,
    proj_output,
    query_feats,
    example_slot,
):
    tokens, width = hidden_in.shape
    depth, feats = value_weight.shape
    proj = proj_input.shape[1]
    lines = proj * proj // 128
    examples = lax.axis_size(DP)
    group = lax.axis_size(FSDP)
    near = group // 2
    across = lax.axis_size("x")
    piece = depth // across
    zhi = lax.axis_index("zhi").astype(jnp.int32).reshape(1)
    spot = jnp.concatenate([lax.axis_index("x").astype(jnp.int32).reshape(1), zhi])
    weight_near = lax.all_gather(value_weight, NEAR, axis=0)
    low = lax.axis_size("zlo")
    mirror = [
        (2 * at + half, 2 * (low - 1 - at) + 1 - half) for at in range(low) for half in range(2)
    ]
    gain = jnp.broadcast_to(norm_gain[None], (16, depth))
    rows = lax.dynamic_slice_in_dim(value_weight, lax.axis_index("x") * piece, piece, 0)
    send = jnp.concatenate([proj_input.T, gain, rows], axis=0)
    recv = lax.ppermute(send, ("zlo", "zhi"), mirror)

    inv, right = pl.pallas_call(
        token_stats,
        out_shape=(shape((tokens, 128), F32), shape((tokens, proj), BF16)),
        in_specs=[VMEM] * 3,
        out_specs=(VMEM, VMEM),
        compiler_params=PARAMS,
        cost_estimate=cost(2 * tokens * width, 2 * tokens * width),
    )(hidden_in, value_grad, proj_output.T)
    recv, inv, right = lax.optimization_barrier((recv, inv, right))
    rows_far = recv[proj + 16 :]

    def folded(part):
        return (part[:proj].astype(F32) * part[proj : proj + 1].astype(F32)).astype(BF16)

    pair = jnp.concatenate(
        [folded(send), folded(recv), send[proj : proj + 8], recv[proj : proj + 8]], axis=0
    )
    pairs = lax.all_to_all(
        jnp.broadcast_to(pair[None], (near,) + pair.shape), NEAR, 0, 0, tiled=True
    )
    moved = [rows_far] + [
        lax.ppermute(rows_far, "x", [(i, (i + hop) % across) for i in range(across)])
        for hop in range(1, across)
    ]
    moved, pairs = lax.optimization_barrier((moved, pairs))
    weight_far = lax.all_gather(jnp.concatenate(moved, axis=0), NEAR, axis=0)

    partial = pl.pallas_call(
        partial_feats,
        out_shape=shape((lines, 128), F32),
        in_specs=[SMEM] + [VMEM] * 4,
        out_specs=VMEM,
        scratch_shapes=[pltpu.VMEM((proj, proj), F32)],
        compiler_params=PARAMS,
    )(zhi, hidden_in, pairs, inv, right)
    partials = lax.all_to_all(
        jnp.broadcast_to(partial.astype(BF16)[None], (group, lines, 128)), FSDP, 0, 0, tiled=True
    )
    own = jnp.sum(partials.astype(F32), axis=0).astype(BF16)
    table = lax.all_to_all(
        jnp.broadcast_to(own[None], (examples, lines, 128)), DP, 0, 0, tiled=True
    )
    _, weight_near = lax.optimization_barrier((own, weight_near))
    near_scaled, near_inner = pl.pallas_call(
        near_half,
        out_shape=(shape((near, tokens, depth), BF16), shape((tokens, 128), F32)),
        in_specs=[SMEM] + [VMEM] * 3 + [HBM],
        out_specs=(VMEM, VMEM),
        scratch_shapes=[
            pltpu.VMEM((near, depth, feats), BF16),
            pltpu.SemaphoreType.DMA((near,)),
        ],
        compiler_params=LARGE,
        cost_estimate=cost(tokens * feats * width, feats * width),
    )(spot, hidden_in, value_grad, pairs, weight_near)
    weight_far, near_inner = lax.optimization_barrier((weight_far, near_inner))
    input_grad = pl.pallas_call(
        input_gradient,
        out_shape=shape((tokens, width), BF16),
        in_specs=[SMEM] + [VMEM] * 3 + [HBM] + [VMEM] * 3,
        out_specs=HBM,
        scratch_shapes=[
            pltpu.VMEM((near, depth, feats), BF16),
            pltpu.SemaphoreType.DMA((near,)),
            pltpu.VMEM((near, tokens, depth), F32),
            pltpu.VMEM((group, tokens, depth), BF16),
            pltpu.SemaphoreType.DMA((group,)),
        ],
        compiler_params=LARGE,
        cost_estimate=cost(tokens * feats * width, 2 * feats * width),
    )(spot, hidden_in, value_grad, pairs, weight_far, near_scaled, near_inner, inv)

    table, input_grad = lax.optimization_barrier((table, input_grad))
    place = jnp.stack([lax.axis_index(DP), lax.axis_index(FSDP)]).astype(jnp.int32)
    gram, score = pl.pallas_call(
        finish,
        out_shape=(
            shape((proj * proj // examples, proj * proj // group), F32),
            shape((query_feats.shape[0], examples), F32),
        ),
        in_specs=[SMEM] + [VMEM] * 3,
        out_specs=(VMEM, VMEM),
        scratch_shapes=[pltpu.VMEM((examples, lines, 128), F32)],
        compiler_params=PARAMS,
    )(place, table, query_feats.reshape(-1, lines, 128), example_slot.reshape(examples, 1))

    return (input_grad, gram, score.T)


def solution(mesh):
    fine = Mesh(mesh.devices.reshape(8, 4, 2, 4, 2), NAMES)
    return jax.shard_map(
        local,
        mesh=fine,
        in_specs=(
            P(NAMES, None),
            P(FSDP),
            P(NAMES, None),
            P(FSDP, None),
            P(FSDP, None),
            P(),
            P(NAMES, None),
            P(),
        ),
        out_specs=(P(NAMES, None), P(DP, FSDP), P(None, NAMES)),
        check_vma=False,
    )
```

```python
import jax
import jax.numpy as jnp
from jax import lax
from jax.experimental import pallas as pl
from jax.experimental.pallas import tpu as pltpu
from jax.sharding import Mesh, PartitionSpec as P

F32 = jnp.float32
BF16 = jnp.bfloat16

NAMES = ("zlo", "x", "zhi", "y", "core")
DP = ("zlo", "x")
FSDP = ("zhi", "y", "core")
NEAR = ("y", "core")

NT = (((1,), (1,)), ((), ()))
TN = (((0,), (0,)), ((), ()))
VMEM = pl.BlockSpec(memory_space=pltpu.VMEM)
SMEM = pl.BlockSpec(memory_space=pltpu.SMEM)
HBM = pl.BlockSpec(memory_space=pltpu.HBM)
LARGE = pltpu.CompilerParams(vmem_limit_bytes=56 * 1024 * 1024)
PARAMS = pltpu.CompilerParams(vmem_limit_bytes=24 * 1024 * 1024)


def shape(dims, dtype):
    return jax.ShapeDtypeStruct(dims, dtype)


def cost(flops, traffic):
    return pl.CostEstimate(flops=flops, bytes_accessed=traffic, transcendentals=0)


def lane_sum(value):
    total = value[:, :128]
    for at in range(128, value.shape[1], 128):
        total = total + value[:, at : at + 128]
    return total


def token_stats(x_ref, v_ref, po_ref, inv_ref, right_ref):
    rows, width = x_ref.shape
    step = 512

    def body(at, acc):
        part = x_ref[:, pl.ds(pl.multiple_of(at * step, step), step)].astype(F32)
        return acc + lane_sum(part * part)

    acc = lax.fori_loop(0, width // step, body, jnp.zeros((rows, 128), F32))
    mean = jnp.sum(acc, axis=1, keepdims=True) / width
    inv_ref[...] = jnp.broadcast_to(lax.rsqrt(mean + 1e-05), inv_ref.shape)
    right_ref[...] = lax.dot_general(
        v_ref[...], po_ref[...], NT, preferred_element_type=F32
    ).astype(BF16)


def partial_feats(zhi_ref, x_ref, g_ref, inv_ref, right_ref, out_ref, rows_ref):
    near, both, depth = g_ref.shape
    proj = (both - 16) // 2
    zhi = zhi_ref[0]
    acc = jnp.zeros((x_ref.shape[0], proj), F32)
    for half in range(2):
        first = (zhi if half == 0 else 1 - zhi) * near
        for at in range(near):
            cols = pl.ds(pl.multiple_of((first + at) * depth, depth), depth)
            acc = acc + lax.dot_general(
                x_ref[:, cols], g_ref[at, half * proj : (half + 1) * proj, :], NT,
                preferred_element_type=F32,
            )
    left = (acc * inv_ref[:, :1]).astype(BF16)
    rows_ref[...] = lax.dot_general(left, right_ref[...], TN, preferred_element_type=F32)
    even = rows_ref[pl.ds(0, proj // 2, stride=2), :]
    odd = rows_ref[pl.ds(1, proj // 2, stride=2), :]
    out_ref[...] = jnp.concatenate([even, odd], axis=1)


def finish(place_ref, tab_ref, q_ref, slot_ref, gram_ref, score_ref, wide_ref):
    count = tab_ref.shape[0]
    wide_ref[...] = tab_ref[...].astype(F32)
    row, col = place_ref[0], place_ref[1]
    rows = wide_ref[:, row, :].astype(BF16)
    for k in range(2):
        cols = wide_ref[:, 2 * col + k, :].astype(BF16)
        gram_ref[:, k * 128 : (k + 1) * 128] = lax.dot_general(
            rows, cols, TN, preferred_element_type=F32
        )
    hit = slot_ref[...] == lax.broadcasted_iota(jnp.int32, (count, count), 1)
    for k in range(q_ref.shape[0]):
        terms = jnp.sum(wide_ref[...] * q_ref[k][None], axis=1)
        raw = jnp.sum(terms, axis=1, keepdims=True)
        score_ref[k : k + 1, :] = jnp.sum(jnp.where(hit, raw, 0.0), axis=0, keepdims=True)


def half_product(first, order, x_ref, v_ref, w_ref, g_ref, row, s_ref, held_ref, sem, acc):
    near, depth, _ = w_ref.shape
    copies = [
        pltpu.make_async_copy(w_ref.at[at], held_ref.at[at], sem.at[at]) for at in range(near)
    ]
    for copy in copies:
        copy.start()
    for at in range(near):
        copies[at].wait()
        product = lax.dot_general(v_ref[...], held_ref[at], NT, preferred_element_type=F32)
        for k in range(depth // 128):
            part = order[k] * 128
            part = part if isinstance(part, int) else pl.multiple_of(part, 128)
            gain = g_ref[at, row : row + 8, pl.ds(part, 128)][:1].astype(F32)
            scaled = product[:, k * 128 : (k + 1) * 128] * gain
            s_ref[at, :, pl.ds(part, 128)] = scaled.astype(s_ref.dtype)
            cols = pl.ds(pl.multiple_of((first + at) * depth + part, 128), 128)
            acc = acc + scaled * x_ref[:, cols].astype(F32)
    return acc


def near_half(spot_ref, x_ref, v_ref, g_ref, w_ref, s_ref, inner_ref, held_ref, sem):
    near, depth, _ = w_ref.shape
    inner_ref[...] = half_product(
        spot_ref[1] * near, range(depth // 128), x_ref, v_ref, w_ref, g_ref, g_ref.shape[1] - 16,
        s_ref, held_ref, sem, jnp.zeros(inner_ref.shape, F32),
    )


def input_gradient(
    spot_ref, x_ref, v_ref, g_ref, w_ref, s_ref, inner_ref, inv_ref, o_ref,
    held_ref, sem, far_ref, out_ref, out_sem,
):
    near, depth, _ = w_ref.shape
    width = x_ref.shape[1]
    across = depth // 128
    zhi = spot_ref[1]
    turn = [lax.rem(spot_ref[0] - hop + across, across) for hop in range(across)]
    acc = half_product(
        (1 - zhi) * near, turn, x_ref, v_ref, w_ref, g_ref, g_ref.shape[1] - 8,
        far_ref, held_ref, sem, inner_ref[...],
    )
    inv = inv_ref[...]
    total = jnp.broadcast_to(jnp.sum(acc, axis=1, keepdims=True), inv.shape)
    factor = total * inv * inv * inv / width
    stores = []
    for slot in range(2 * near):
        half, at = divmod(slot, near)
        source = s_ref if half == 0 else far_ref
        first = ((zhi if half == 0 else 1 - zhi) * near + at) * depth
        cols = pl.ds(pl.multiple_of(first, depth), depth)
        for k in range(across):
            here = slice(k * 128, (k + 1) * 128)
            some = pl.ds(pl.multiple_of(first + k * 128, 128), 128)
            out_ref[slot, :, here] = (
                source[at, :, here].astype(F32) * inv - x_ref[:, some].astype(F32) * factor
            ).astype(BF16)
        copy = pltpu.make_async_copy(out_ref.at[slot], o_ref.at[:, cols], out_sem.at[slot])
        copy.start()
        stores.append(copy)
    for copy in stores:
        copy.wait()


def local(
    hidden_in,
    norm_gain,
    value_grad,
    value_weight,
    proj_input,
    proj_output,
    query_feats,
    example_slot,
):
    tokens, width = hidden_in.shape
    depth, feats = value_weight.shape
    proj = proj_input.shape[1]
    lines = proj * proj // 128
    examples = lax.axis_size(DP)
    group = lax.axis_size(FSDP)
    near = group // 2
    across = lax.axis_size("x")
    piece = depth // across
    zhi = lax.axis_index("zhi").astype(jnp.int32).reshape(1)
    spot = jnp.concatenate([lax.axis_index("x").astype(jnp.int32).reshape(1), zhi])
    weight_near = lax.all_gather(value_weight, NEAR, axis=0)
    low = lax.axis_size("zlo")
    mirror = [
        (2 * at + half, 2 * (low - 1 - at) + 1 - half) for at in range(low) for half in range(2)
    ]
    gain = jnp.broadcast_to(norm_gain[None], (16, depth))
    rows = lax.dynamic_slice_in_dim(value_weight, lax.axis_index("x") * piece, piece, 0)
    send = jnp.concatenate([proj_input.T, gain, rows], axis=0)
    recv = lax.ppermute(send, ("zlo", "zhi"), mirror)

    inv, right = pl.pallas_call(
        token_stats,
        out_shape=(shape((tokens, 128), F32), shape((tokens, proj), BF16)),
        in_specs=[VMEM] * 3,
        out_specs=(VMEM, VMEM),
        compiler_params=PARAMS,
        cost_estimate=cost(2 * tokens * width, 2 * tokens * width),
    )(hidden_in, value_grad, proj_output.T)
    recv, inv, right = lax.optimization_barrier((recv, inv, right))
    rows_far = recv[proj + 16 :]

    def folded(part):
        return (part[:proj].astype(F32) * part[proj : proj + 1].astype(F32)).astype(BF16)

    pair = jnp.concatenate(
        [folded(send), folded(recv), send[proj : proj + 8], recv[proj : proj + 8]], axis=0
    )
    pairs = lax.all_to_all(
        jnp.broadcast_to(pair[None], (near,) + pair.shape), NEAR, 0, 0, tiled=True
    )
    moved = [rows_far] + [
        lax.ppermute(rows_far, "x", [(i, (i + hop) % across) for i in range(across)])
        for hop in range(1, across)
    ]
    shard_far = jnp.concatenate(moved, axis=0)
    shard_far, pairs = lax.optimization_barrier((shard_far, pairs))
    weight_far = lax.all_gather(shard_far, NEAR, axis=0)

    partial = pl.pallas_call(
        partial_feats,
        out_shape=shape((lines, 128), F32),
        in_specs=[SMEM] + [VMEM] * 4,
        out_specs=VMEM,
        scratch_shapes=[pltpu.VMEM((proj, proj), F32)],
        compiler_params=PARAMS,
    )(zhi, hidden_in, pairs, inv, right)
    partials = lax.all_to_all(
        jnp.broadcast_to(partial.astype(BF16)[None], (group, lines, 128)), FSDP, 0, 0, tiled=True
    )
    own = jnp.sum(partials.astype(F32), axis=0).astype(BF16)
    table = lax.all_to_all(
        jnp.broadcast_to(own[None], (examples, lines, 128)), DP, 0, 0, tiled=True
    )
    _, weight_near = lax.optimization_barrier((own, weight_near))
    near_scaled, near_inner = pl.pallas_call(
        near_half,
        out_shape=(shape((near, tokens, depth), BF16), shape((tokens, 128), F32)),
        in_specs=[SMEM] + [VMEM] * 3 + [HBM],
        out_specs=(VMEM, VMEM),
        scratch_shapes=[
            pltpu.VMEM((near, depth, feats), BF16),
            pltpu.SemaphoreType.DMA((near,)),
        ],
        compiler_params=LARGE,
        cost_estimate=cost(tokens * feats * width, feats * width),
    )(spot, hidden_in, value_grad, pairs, weight_near)
    weight_far, near_inner = lax.optimization_barrier((weight_far, near_inner))
    input_grad = pl.pallas_call(
        input_gradient,
        out_shape=shape((tokens, width), BF16),
        in_specs=[SMEM] + [VMEM] * 3 + [HBM] + [VMEM] * 3,
        out_specs=HBM,
        scratch_shapes=[
            pltpu.VMEM((near, depth, feats), BF16),
            pltpu.SemaphoreType.DMA((near,)),
            pltpu.VMEM((near, tokens, depth), F32),
            pltpu.VMEM((group, tokens, depth), BF16),
            pltpu.SemaphoreType.DMA((group,)),
        ],
        compiler_params=LARGE,
        cost_estimate=cost(tokens * feats * width, 2 * feats * width),
    )(spot, hidden_in, value_grad, pairs, weight_far, near_scaled, near_inner, inv)

    table, input_grad = lax.optimization_barrier((table, input_grad))
    place = jnp.stack([lax.axis_index(DP), lax.axis_index(FSDP)]).astype(jnp.int32)
    gram, score = pl.pallas_call(
        finish,
        out_shape=(
            shape((proj * proj // examples, proj * proj // group), F32),
            shape((query_feats.shape[0], examples), F32),
        ),
        in_specs=[SMEM] + [VMEM] * 3,
        out_specs=(VMEM, VMEM),
        scratch_shapes=[pltpu.VMEM((examples, lines, 128), F32)],
        compiler_params=PARAMS,
    )(place, table, query_feats.reshape(-1, lines, 128), example_slot.reshape(examples, 1))

    return (input_grad, gram, score.T)


def solution(mesh):
    fine = Mesh(mesh.devices.reshape(8, 4, 2, 4, 2), NAMES)
    return jax.shard_map(
        local,
        mesh=fine,
        in_specs=(
            P(NAMES, None),
            P(FSDP),
            P(NAMES, None),
            P(FSDP, None),
            P(FSDP, None),
            P(),
            P(NAMES, None),
            P(),
        ),
        out_specs=(P(NAMES, None), P(DP, FSDP), P(None, NAMES)),
        check_vma=False,
    )
```

```python
import jax
import jax.numpy as jnp
from jax import lax
from jax.experimental import pallas as pl
from jax.experimental.pallas import tpu as pltpu
from jax.sharding import Mesh, PartitionSpec as P

F32 = jnp.float32
BF16 = jnp.bfloat16

NAMES = ("zlo", "x", "zhi", "y", "core")
DP = ("zlo", "x")
FSDP = ("zhi", "y", "core")
NEAR = ("y", "core")

NT = (((1,), (1,)), ((), ()))
TN = (((0,), (0,)), ((), ()))
VMEM = pl.BlockSpec(memory_space=pltpu.VMEM)
SMEM = pl.BlockSpec(memory_space=pltpu.SMEM)
HBM = pl.BlockSpec(memory_space=pltpu.HBM)
LARGE = pltpu.CompilerParams(vmem_limit_bytes=56 * 1024 * 1024)
PARAMS = pltpu.CompilerParams(vmem_limit_bytes=24 * 1024 * 1024)


def shape(dims, dtype):
    return jax.ShapeDtypeStruct(dims, dtype)


def cost(flops, traffic):
    return pl.CostEstimate(flops=flops, bytes_accessed=traffic, transcendentals=0)


def lane_sum(value):
    total = value[:, :128]
    for at in range(128, value.shape[1], 128):
        total = total + value[:, at : at + 128]
    return total


def token_stats(x_ref, v_ref, po_ref, inv_ref, right_ref):
    rows, width = x_ref.shape
    step = 512

    def body(at, acc):
        part = x_ref[:, pl.ds(pl.multiple_of(at * step, step), step)].astype(F32)
        return acc + lane_sum(part * part)

    acc = lax.fori_loop(0, width // step, body, jnp.zeros((rows, 128), F32))
    mean = jnp.sum(acc, axis=1, keepdims=True) / width
    inv_ref[...] = jnp.broadcast_to(lax.rsqrt(mean + 1e-05), inv_ref.shape)
    right_ref[...] = lax.dot_general(
        v_ref[...], po_ref[...], NT, preferred_element_type=F32
    ).astype(BF16)


def partial_feats(place_ref, x_ref, same_ref, other_ref, inv_ref, right_ref, out_ref, rows_ref):
    chips, both, depth = same_ref.shape
    proj = (both - 16) // 2
    zhi, core = place_ref[0], place_ref[1]
    acc = jnp.zeros((x_ref.shape[0], proj), F32)
    for half in range(2):
        first = (zhi if half == 0 else 1 - zhi) * 2 * chips
        for which, source in ((core, same_ref), (1 - core, other_ref)):
            for at in range(chips):
                start = (first + 2 * at + which) * depth
                cols = pl.ds(pl.multiple_of(start, depth), depth)
                acc = acc + lax.dot_general(
                    x_ref[:, cols], source[at, half * proj : (half + 1) * proj, :], NT,
                    preferred_element_type=F32,
                )
    left = (acc * inv_ref[:, :1]).astype(BF16)
    rows_ref[...] = lax.dot_general(left, right_ref[...], TN, preferred_element_type=F32)
    even = rows_ref[pl.ds(0, proj // 2, stride=2), :]
    odd = rows_ref[pl.ds(1, proj // 2, stride=2), :]
    out_ref[...] = jnp.concatenate([even, odd], axis=1)


def finish(place_ref, tab_ref, q_ref, slot_ref, gram_ref, score_ref, wide_ref):
    count = tab_ref.shape[0]
    wide_ref[...] = tab_ref[...].astype(F32)
    row, col = place_ref[0], place_ref[1]
    rows = wide_ref[:, row, :].astype(BF16)
    for k in range(2):
        cols = wide_ref[:, 2 * col + k, :].astype(BF16)
        gram_ref[:, k * 128 : (k + 1) * 128] = lax.dot_general(
            rows, cols, TN, preferred_element_type=F32
        )
    hit = slot_ref[...] == lax.broadcasted_iota(jnp.int32, (count, count), 1)
    for k in range(q_ref.shape[0]):
        terms = jnp.sum(wide_ref[...] * q_ref[k][None], axis=1)
        raw = jnp.sum(terms, axis=1, keepdims=True)
        score_ref[k : k + 1, :] = jnp.sum(jnp.where(hit, raw, 0.0), axis=0, keepdims=True)


def half_product(first, order, x_ref, v_ref, w_ref, g_ref, row, s_ref, held_ref, sem, acc):
    near, depth, _ = w_ref.shape
    copies = [
        pltpu.make_async_copy(w_ref.at[at], held_ref.at[at], sem.at[at]) for at in range(near)
    ]
    for copy in copies:
        copy.start()
    for at in range(near):
        copies[at].wait()
        product = lax.dot_general(v_ref[...], held_ref[at], NT, preferred_element_type=F32)
        for k in range(depth // 128):
            part = order[k] * 128
            part = part if isinstance(part, int) else pl.multiple_of(part, 128)
            gain = g_ref[at, row : row + 8, pl.ds(part, 128)][:1].astype(F32)
            scaled = product[:, k * 128 : (k + 1) * 128] * gain
            s_ref[at, :, pl.ds(part, 128)] = scaled.astype(s_ref.dtype)
            cols = pl.ds(pl.multiple_of((first + at) * depth + part, 128), 128)
            acc = acc + scaled * x_ref[:, cols].astype(F32)
    return acc


def near_half(spot_ref, x_ref, v_ref, g_ref, w_ref, s_ref, inner_ref, held_ref, sem):
    near, depth, _ = w_ref.shape
    inner_ref[...] = half_product(
        spot_ref[1] * near, range(depth // 128), x_ref, v_ref, w_ref, g_ref, g_ref.shape[1] - 16,
        s_ref, held_ref, sem, jnp.zeros(inner_ref.shape, F32),
    )


def input_gradient(
    spot_ref, x_ref, v_ref, g_ref, w_ref, s_ref, inner_ref, inv_ref, o_ref,
    held_ref, sem, far_ref, out_ref, out_sem,
):
    near, depth, _ = w_ref.shape
    width = x_ref.shape[1]
    across = depth // 128
    zhi = spot_ref[1]
    turn = [lax.rem(spot_ref[0] - hop + across, across) for hop in range(across)]
    acc = half_product(
        (1 - zhi) * near, turn, x_ref, v_ref, w_ref, g_ref, g_ref.shape[1] - 8,
        far_ref, held_ref, sem, inner_ref[...],
    )
    inv = inv_ref[...]
    total = jnp.broadcast_to(jnp.sum(acc, axis=1, keepdims=True), inv.shape)
    factor = total * inv * inv * inv / width
    stores = []
    for slot in range(2 * near):
        half, at = divmod(slot, near)
        source = s_ref if half == 0 else far_ref
        first = ((zhi if half == 0 else 1 - zhi) * near + at) * depth
        cols = pl.ds(pl.multiple_of(first, depth), depth)
        for k in range(across):
            here = slice(k * 128, (k + 1) * 128)
            some = pl.ds(pl.multiple_of(first + k * 128, 128), 128)
            out_ref[slot, :, here] = (
                source[at, :, here].astype(F32) * inv - x_ref[:, some].astype(F32) * factor
            ).astype(BF16)
        copy = pltpu.make_async_copy(out_ref.at[slot], o_ref.at[:, cols], out_sem.at[slot])
        copy.start()
        stores.append(copy)
    for copy in stores:
        copy.wait()


def local(
    hidden_in,
    norm_gain,
    value_grad,
    value_weight,
    proj_input,
    proj_output,
    query_feats,
    example_slot,
):
    tokens, width = hidden_in.shape
    depth, feats = value_weight.shape
    proj = proj_input.shape[1]
    lines = proj * proj // 128
    examples = lax.axis_size(DP)
    group = lax.axis_size(FSDP)
    near = group // 2
    across = lax.axis_size("x")
    piece = depth // across
    zhi = lax.axis_index("zhi").astype(jnp.int32).reshape(1)
    spot = jnp.concatenate([lax.axis_index("x").astype(jnp.int32).reshape(1), zhi])
    weight_near = lax.all_gather(value_weight, NEAR, axis=0)
    low = lax.axis_size("zlo")
    mirror = [
        (2 * at + half, 2 * (low - 1 - at) + 1 - half) for at in range(low) for half in range(2)
    ]
    gain = jnp.broadcast_to(norm_gain[None], (16, depth))
    rows = lax.dynamic_slice_in_dim(value_weight, lax.axis_index("x") * piece, piece, 0)
    send = jnp.concatenate([proj_input.T, gain, rows], axis=0)
    recv = lax.ppermute(send, ("zlo", "zhi"), mirror)

    inv, right = pl.pallas_call(
        token_stats,
        out_shape=(shape((tokens, 128), F32), shape((tokens, proj), BF16)),
        in_specs=[VMEM] * 3,
        out_specs=(VMEM, VMEM),
        compiler_params=PARAMS,
        cost_estimate=cost(2 * tokens * width, 2 * tokens * width),
    )(hidden_in, value_grad, proj_output.T)
    recv, inv, right = lax.optimization_barrier((recv, inv, right))
    rows_far = recv[proj + 16 :]

    def folded(part):
        return (part[:proj].astype(F32) * part[proj : proj + 1].astype(F32)).astype(BF16)

    pair = jnp.concatenate(
        [folded(send), folded(recv), send[proj : proj + 8], recv[proj : proj + 8]], axis=0
    )
    same = lax.all_to_all(
        jnp.broadcast_to(pair[None], (near // 2,) + pair.shape), "y", 0, 0, tiled=True
    )
    moved = [rows_far] + [
        lax.ppermute(rows_far, "x", [(i, (i + hop) % across) for i in range(across)])
        for hop in range(1, across)
    ]
    shard_far = jnp.concatenate(moved, axis=0)
    shard_far, same = lax.optimization_barrier((shard_far, same))
    weight_far = lax.all_gather(shard_far, NEAR, axis=0)
    other = lax.ppermute(same, "core", [(0, 1), (1, 0)])
    core = lax.axis_index("core")
    gains = [part[:, 2 * proj :] for part in (same, other)]
    first = [jnp.where(core == 0, gains[k], gains[1 - k]) for k in range(2)]
    gains = jnp.stack(first, axis=1).reshape(near, 16, depth)
    place_core = jnp.concatenate([zhi, core.astype(jnp.int32).reshape(1)])

    partial = pl.pallas_call(
        partial_feats,
        out_shape=shape((lines, 128), F32),
        in_specs=[SMEM] + [VMEM] * 5,
        out_specs=VMEM,
        scratch_shapes=[pltpu.VMEM((proj, proj), F32)],
        compiler_params=PARAMS,
    )(place_core, hidden_in, same, other, inv, right)
    partials = lax.all_to_all(
        jnp.broadcast_to(partial.astype(BF16)[None], (group, lines, 128)), FSDP, 0, 0, tiled=True
    )
    own = jnp.sum(partials.astype(F32), axis=0).astype(BF16)
    table = lax.all_to_all(
        jnp.broadcast_to(own[None], (examples, lines, 128)), DP, 0, 0, tiled=True
    )
    _, weight_near = lax.optimization_barrier((own, weight_near))
    near_scaled, near_inner = pl.pallas_call(
        near_half,
        out_shape=(shape((near, tokens, depth), BF16), shape((tokens, 128), F32)),
        in_specs=[SMEM] + [VMEM] * 3 + [HBM],
        out_specs=(VMEM, VMEM),
        scratch_shapes=[
            pltpu.VMEM((near, depth, feats), BF16),
            pltpu.SemaphoreType.DMA((near,)),
        ],
        compiler_params=LARGE,
        cost_estimate=cost(tokens * feats * width, feats * width),
    )(spot, hidden_in, value_grad, gains, weight_near)
    weight_far, near_inner = lax.optimization_barrier((weight_far, near_inner))
    input_grad = pl.pallas_call(
        input_gradient,
        out_shape=shape((tokens, width), BF16),
        in_specs=[SMEM] + [VMEM] * 3 + [HBM] + [VMEM] * 3,
        out_specs=HBM,
        scratch_shapes=[
            pltpu.VMEM((near, depth, feats), BF16),
            pltpu.SemaphoreType.DMA((near,)),
            pltpu.VMEM((near, tokens, depth), F32),
            pltpu.VMEM((group, tokens, depth), BF16),
            pltpu.SemaphoreType.DMA((group,)),
        ],
        compiler_params=LARGE,
        cost_estimate=cost(tokens * feats * width, 2 * feats * width),
    )(spot, hidden_in, value_grad, gains, weight_far, near_scaled, near_inner, inv)

    table, input_grad = lax.optimization_barrier((table, input_grad))
    place = jnp.stack([lax.axis_index(DP), lax.axis_index(FSDP)]).astype(jnp.int32)
    gram, score = pl.pallas_call(
        finish,
        out_shape=(
            shape((proj * proj // examples, proj * proj // group), F32),
            shape((query_feats.shape[0], examples), F32),
        ),
        in_specs=[SMEM] + [VMEM] * 3,
        out_specs=(VMEM, VMEM),
        scratch_shapes=[pltpu.VMEM((examples, lines, 128), F32)],
        compiler_params=PARAMS,
    )(place, table, query_feats.reshape(-1, lines, 128), example_slot.reshape(examples, 1))

    return (input_grad, gram, score.T)


def solution(mesh):
    fine = Mesh(mesh.devices.reshape(8, 4, 2, 4, 2), NAMES)
    return jax.shard_map(
        local,
        mesh=fine,
        in_specs=(
            P(NAMES, None),
            P(FSDP),
            P(NAMES, None),
            P(FSDP, None),
            P(FSDP, None),
            P(),
            P(NAMES, None),
            P(),
        ),
        out_specs=(P(NAMES, None), P(DP, FSDP), P(None, NAMES)),
        check_vma=False,
    )
```

```python
import jax
import jax.numpy as jnp
from jax import lax
from jax.experimental import pallas as pl
from jax.experimental.pallas import tpu as pltpu
from jax.sharding import Mesh, PartitionSpec as P

F32 = jnp.float32
BF16 = jnp.bfloat16

NAMES = ("zlo", "x", "zhi", "y", "core")
DP = ("zlo", "x")
FSDP = ("zhi", "y", "core")
NEAR = ("y", "core")

NT = (((1,), (1,)), ((), ()))
TN = (((0,), (0,)), ((), ()))
VMEM = pl.BlockSpec(memory_space=pltpu.VMEM)
SMEM = pl.BlockSpec(memory_space=pltpu.SMEM)
HBM = pl.BlockSpec(memory_space=pltpu.HBM)
LARGE = pltpu.CompilerParams(vmem_limit_bytes=56 * 1024 * 1024)
PARAMS = pltpu.CompilerParams(vmem_limit_bytes=24 * 1024 * 1024)


def shape(dims, dtype):
    return jax.ShapeDtypeStruct(dims, dtype)


def cost(flops, traffic):
    return pl.CostEstimate(flops=flops, bytes_accessed=traffic, transcendentals=0)


def lane_sum(value):
    total = value[:, :128]
    for at in range(128, value.shape[1], 128):
        total = total + value[:, at : at + 128]
    return total


def token_stats(x_ref, v_ref, po_ref, inv_ref, right_ref):
    rows, width = x_ref.shape
    step = 512

    def body(at, acc):
        part = x_ref[:, pl.ds(pl.multiple_of(at * step, step), step)].astype(F32)
        return acc + lane_sum(part * part)

    acc = lax.fori_loop(0, width // step, body, jnp.zeros((rows, 128), F32))
    mean = jnp.sum(acc, axis=1, keepdims=True) / width
    inv_ref[...] = jnp.broadcast_to(lax.rsqrt(mean + 1e-05), inv_ref.shape)
    right_ref[...] = lax.dot_general(
        v_ref[...], po_ref[...], NT, preferred_element_type=F32
    ).astype(BF16)


def partial_feats(place_ref, x_ref, same_ref, other_ref, inv_ref, right_ref, out_ref, rows_ref):
    chips, both, depth = same_ref.shape
    proj = (both - 16) // 2
    zhi, core = place_ref[0], place_ref[1]
    acc = jnp.zeros((x_ref.shape[0], proj), F32)
    for half in range(2):
        first = (zhi if half == 0 else 1 - zhi) * 2 * chips
        for which, source in ((core, same_ref), (1 - core, other_ref)):
            for at in range(chips):
                start = (first + 2 * at + which) * depth
                cols = pl.ds(pl.multiple_of(start, depth), depth)
                acc = acc + lax.dot_general(
                    x_ref[:, cols], source[at, half * proj : (half + 1) * proj, :], NT,
                    preferred_element_type=F32,
                )
    left = (acc * inv_ref[:, :1]).astype(BF16)
    rows_ref[...] = lax.dot_general(left, right_ref[...], TN, preferred_element_type=F32)
    even = rows_ref[pl.ds(0, proj // 2, stride=2), :]
    odd = rows_ref[pl.ds(1, proj // 2, stride=2), :]
    out_ref[...] = jnp.concatenate([even, odd], axis=1)


def finish(place_ref, tab_ref, q_ref, slot_ref, gram_ref, score_ref, wide_ref):
    count = tab_ref.shape[0]
    wide_ref[...] = tab_ref[...].astype(F32)
    row, col = place_ref[0], place_ref[1]
    rows = wide_ref[:, row, :].astype(BF16)
    for k in range(2):
        cols = wide_ref[:, 2 * col + k, :].astype(BF16)
        gram_ref[:, k * 128 : (k + 1) * 128] = lax.dot_general(
            rows, cols, TN, preferred_element_type=F32
        )
    hit = slot_ref[...] == lax.broadcasted_iota(jnp.int32, (count, count), 1)
    for k in range(q_ref.shape[0]):
        terms = jnp.sum(wide_ref[...] * q_ref[k][None], axis=1)
        raw = jnp.sum(terms, axis=1, keepdims=True)
        score_ref[k : k + 1, :] = jnp.sum(jnp.where(hit, raw, 0.0), axis=0, keepdims=True)


def half_product(first, order, x_ref, v_ref, w_ref, g_ref, row, s_ref, held_ref, sem, acc):
    near, depth, _ = w_ref.shape
    copies = [
        pltpu.make_async_copy(w_ref.at[at], held_ref.at[at], sem.at[at]) for at in range(near)
    ]
    for copy in copies:
        copy.start()
    for at in range(near):
        copies[at].wait()
        product = lax.dot_general(v_ref[...], held_ref[at], NT, preferred_element_type=F32)
        for k in range(depth // 128):
            part = order[k] * 128
            part = part if isinstance(part, int) else pl.multiple_of(part, 128)
            gain = g_ref[at, row : row + 8, pl.ds(part, 128)][:1].astype(F32)
            scaled = product[:, k * 128 : (k + 1) * 128] * gain
            s_ref[at, :, pl.ds(part, 128)] = scaled.astype(s_ref.dtype)
            cols = pl.ds(pl.multiple_of((first + at) * depth + part, 128), 128)
            acc = acc + scaled * x_ref[:, cols].astype(F32)
    return acc


def near_half(spot_ref, x_ref, v_ref, g_ref, w_ref, s_ref, inner_ref, held_ref, sem):
    near, depth, _ = w_ref.shape
    inner_ref[...] = half_product(
        spot_ref[1] * near, range(depth // 128), x_ref, v_ref, w_ref, g_ref, g_ref.shape[1] - 16,
        s_ref, held_ref, sem, jnp.zeros(inner_ref.shape, F32),
    )


def input_gradient(
    spot_ref, x_ref, v_ref, g_ref, w_ref, s_ref, inner_ref, inv_ref, o_ref,
    held_ref, sem, far_ref, out_ref, out_sem,
):
    near, depth, _ = w_ref.shape
    width = x_ref.shape[1]
    across = depth // 128
    zhi = spot_ref[1]
    turn = [lax.rem(spot_ref[0] - hop + across, across) for hop in range(across)]
    acc = half_product(
        (1 - zhi) * near, turn, x_ref, v_ref, w_ref, g_ref, g_ref.shape[1] - 8,
        far_ref, held_ref, sem, inner_ref[...],
    )
    inv = inv_ref[...]
    total = jnp.broadcast_to(jnp.sum(acc, axis=1, keepdims=True), inv.shape)
    factor = total * inv * inv * inv / width
    stores = []
    for slot in range(2 * near):
        half, at = divmod(slot, near)
        source = s_ref if half == 0 else far_ref
        first = ((zhi if half == 0 else 1 - zhi) * near + at) * depth
        cols = pl.ds(pl.multiple_of(first, depth), depth)
        for k in range(across):
            here = slice(k * 128, (k + 1) * 128)
            some = pl.ds(pl.multiple_of(first + k * 128, 128), 128)
            out_ref[slot, :, here] = (
                source[at, :, here].astype(F32) * inv - x_ref[:, some].astype(F32) * factor
            ).astype(BF16)
        copy = pltpu.make_async_copy(out_ref.at[slot], o_ref.at[:, cols], out_sem.at[slot])
        copy.start()
        stores.append(copy)
    for copy in stores:
        copy.wait()


def local(
    hidden_in,
    norm_gain,
    value_grad,
    value_weight,
    proj_input,
    proj_output,
    query_feats,
    example_slot,
):
    tokens, width = hidden_in.shape
    depth, feats = value_weight.shape
    proj = proj_input.shape[1]
    lines = proj * proj // 128
    examples = lax.axis_size(DP)
    group = lax.axis_size(FSDP)
    near = group // 2
    across = lax.axis_size("x")
    piece = depth // across
    zhi = lax.axis_index("zhi").astype(jnp.int32).reshape(1)
    spot = jnp.concatenate([lax.axis_index("x").astype(jnp.int32).reshape(1), zhi])
    weight_near = lax.all_gather(value_weight, NEAR, axis=0)
    low = lax.axis_size("zlo")
    mirror = [
        (2 * at + half, 2 * (low - 1 - at) + 1 - half) for at in range(low) for half in range(2)
    ]
    gain = jnp.broadcast_to(norm_gain[None], (16, depth))
    rows = lax.dynamic_slice_in_dim(value_weight, lax.axis_index("x") * piece, piece, 0)
    send = jnp.concatenate([proj_input.T, gain, rows], axis=0)
    recv = lax.ppermute(send, ("zlo", "zhi"), mirror)

    inv, right = pl.pallas_call(
        token_stats,
        out_shape=(shape((tokens, 128), F32), shape((tokens, proj), BF16)),
        in_specs=[VMEM] * 3,
        out_specs=(VMEM, VMEM),
        compiler_params=PARAMS,
        cost_estimate=cost(2 * tokens * width, 2 * tokens * width),
    )(hidden_in, value_grad, proj_output.T)
    recv, inv, right = lax.optimization_barrier((recv, inv, right))
    rows_far = recv[proj + 16 :]

    def folded(part):
        return (part[:proj].astype(F32) * part[proj : proj + 1].astype(F32)).astype(BF16)

    pair = jnp.concatenate(
        [folded(send), folded(recv), send[proj : proj + 8], recv[proj : proj + 8]], axis=0
    )
    same = lax.all_to_all(
        jnp.broadcast_to(pair[None], (near // 2,) + pair.shape), "y", 0, 0, tiled=True
    )
    moved = [rows_far] + [
        lax.ppermute(rows_far, "x", [(i, (i + hop) % across) for i in range(across)])
        for hop in range(1, across)
    ]
    shard_far = jnp.concatenate(moved, axis=0)
    shard_far, _ = lax.optimization_barrier((shard_far, same))
    weight_far = lax.all_gather(shard_far, NEAR, axis=0)
    other = lax.ppermute(same, "core", [(0, 1), (1, 0)])
    core = lax.axis_index("core")
    gains = [part[:, 2 * proj :] for part in (same, other)]
    first = [jnp.where(core == 0, gains[k], gains[1 - k]) for k in range(2)]
    gains = jnp.stack(first, axis=1).reshape(near, 16, depth)
    place_core = jnp.concatenate([zhi, core.astype(jnp.int32).reshape(1)])

    partial = pl.pallas_call(
        partial_feats,
        out_shape=shape((lines, 128), F32),
        in_specs=[SMEM] + [VMEM] * 5,
        out_specs=VMEM,
        scratch_shapes=[pltpu.VMEM((proj, proj), F32)],
        compiler_params=PARAMS,
    )(place_core, hidden_in, same, other, inv, right)
    partials = lax.all_to_all(
        jnp.broadcast_to(partial.astype(BF16)[None], (group, lines, 128)), FSDP, 0, 0, tiled=True
    )
    own = jnp.sum(partials.astype(F32), axis=0).astype(BF16)
    table = lax.all_to_all(
        jnp.broadcast_to(own[None], (examples, lines, 128)), DP, 0, 0, tiled=True
    )
    _, weight_near = lax.optimization_barrier((own, weight_near))
    near_scaled, near_inner = pl.pallas_call(
        near_half,
        out_shape=(shape((near, tokens, depth), BF16), shape((tokens, 128), F32)),
        in_specs=[SMEM] + [VMEM] * 3 + [HBM],
        out_specs=(VMEM, VMEM),
        scratch_shapes=[
            pltpu.VMEM((near, depth, feats), BF16),
            pltpu.SemaphoreType.DMA((near,)),
        ],
        compiler_params=LARGE,
        cost_estimate=cost(tokens * feats * width, feats * width),
    )(spot, hidden_in, value_grad, gains, weight_near)
    weight_far, near_inner = lax.optimization_barrier((weight_far, near_inner))
    input_grad = pl.pallas_call(
        input_gradient,
        out_shape=shape((tokens, width), BF16),
        in_specs=[SMEM] + [VMEM] * 3 + [HBM] + [VMEM] * 3,
        out_specs=HBM,
        scratch_shapes=[
            pltpu.VMEM((near, depth, feats), BF16),
            pltpu.SemaphoreType.DMA((near,)),
            pltpu.VMEM((near, tokens, depth), F32),
            pltpu.VMEM((group, tokens, depth), BF16),
            pltpu.SemaphoreType.DMA((group,)),
        ],
        compiler_params=LARGE,
        cost_estimate=cost(tokens * feats * width, 2 * feats * width),
    )(spot, hidden_in, value_grad, gains, weight_far, near_scaled, near_inner, inv)

    table, input_grad = lax.optimization_barrier((table, input_grad))
    place = jnp.stack([lax.axis_index(DP), lax.axis_index(FSDP)]).astype(jnp.int32)
    gram, score = pl.pallas_call(
        finish,
        out_shape=(
            shape((proj * proj // examples, proj * proj // group), F32),
            shape((query_feats.shape[0], examples), F32),
        ),
        in_specs=[SMEM] + [VMEM] * 3,
        out_specs=(VMEM, VMEM),
        scratch_shapes=[pltpu.VMEM((examples, lines, 128), F32)],
        compiler_params=PARAMS,
    )(place, table, query_feats.reshape(-1, lines, 128), example_slot.reshape(examples, 1))

    return (input_grad, gram, score.T)


def solution(mesh):
    fine = Mesh(mesh.devices.reshape(8, 4, 2, 4, 2), NAMES)
    return jax.shard_map(
        local,
        mesh=fine,
        in_specs=(
            P(NAMES, None),
            P(FSDP),
            P(NAMES, None),
            P(FSDP, None),
            P(FSDP, None),
            P(),
            P(NAMES, None),
            P(),
        ),
        out_specs=(P(NAMES, None), P(DP, FSDP), P(None, NAMES)),
        check_vma=False,
    )
```
